32 devices in a mesh: sta: 8 (over z, x), tpl: 4 (over y, core).
Axes of the slice: x: 2, y: 2, z: 4, core: 2. Of those that a mesh axis runs over, the one named last changes fastest.
Arguments:
- records: bfloat16 [256, 3, 4480], P(('sta', 'tpl')), may hold values from -6 to 6
- templates: bfloat16 [768, 10, 3, 200], P(('sta', 'tpl')), may hold values from -6 to 6
- pick_owner: int32 [768, 10], P(('sta', 'tpl')), may hold values from 0 to 31, all different within a row; in each aligned block of 24 rows (0 to 23, 24 to 47, ...) at most 12 rows name the same one
- pick_local: int32 [768, 10], P(('sta', 'tpl')), may hold values from 0 to 7
- moveout: int32 [768, 10], P(('sta', 'tpl')), may hold values from 0 to 127
- channel_mask: int32 [768, 10, 3], P(('sta', 'tpl')), may hold values 0 or 1
Outputs:
- detection: float32 [768, 4096], P(('sta', 'tpl'))
The draws below stay inside these ranges and needn't reach their ends.
Inputs may be any that keep to these rules, and one draw needn't show every extreme that they name: `pick_owner`: each template names 10 different devices; among the templates of one device no device is named more than 12 times, and some device is named exactly 12 times.
All inputs are finite; a program needn't handle non-finite values. No bound on the sum of `channel_mask` on one device may be relied on, other than what follows from the above.
Results may differ from the reference program's by a relative error of at most 0.0029.
Values may be sent and summed in bfloat16 or wider, within the bound.
A program may use at most 128 MiB of HBM per device.

```python
import math
import jax
import jax.numpy as jnp
import numpy as np
from jax import lax

STA_LOC = 8
TPL_LOC = 24
LAGS = 4096
PICKS = 10
TLEN = 200
DLEN = 4480
CAP = 12
STATIONS = 256
TEMPLATES = 768
DEVICES = 32


def set_ends(values, rng, least, largest):
    longest = values.shape.index(max(values.shape))
    spots = []
    for shift in (0, 1):
        where = [jax.random.randint(jax.random.fold_in(rng, axis), (), 0, length) for axis, length in enumerate(values.shape)]
        where[longest] = (where[longest] + shift) % values.shape[longest]
        spots.append(tuple(where))
    return values.at[spots[0]].set(least).at[spots[1]].set(largest)


def level_of(own_key, dims, cuts, least, top_value):
    gain, own = 1.0, jax.random.fold_in(own_key, 6)
    for axis_at, blocks in cuts:
        steps = jnp.exp(jax.random.uniform(jax.random.fold_in(own, axis_at), (blocks,), jnp.float32, least / len(cuts), top_value / len(cuts)))
        gain = gain * jnp.repeat(steps, dims[axis_at] // blocks).reshape([-1 if axis == axis_at else 1 for axis in range(len(dims))])
    return gain


def routed_block(key, own, number, rows, count, top, limit, lean):
    order = jax.random.permutation(key, count)
    crowded, usual = load_shares(count, rows * top, limit, lean, True), load_shares(count, rows * top, limit, lean, False)
    places = jnp.arange(count)

    def named(tallies, offset_by):
        used = int((tallies > 0).sum())
        fixed = max(1, used // 4)
        shifted = fixed + (places - fixed + offset_by * (used - fixed)) % max(1, count - fixed)
        return jnp.zeros((count,), jnp.int32).at[order[jnp.where(places < fixed, places, shifted)]].set(jnp.asarray(tallies, jnp.int32))

    tallies = jnp.where(number % 4 == 0, named(crowded, number // 4), named(usual, number - number // 4 - 1))
    mixed = jax.random.permutation(jax.random.fold_in(own, 3), count)
    giver, sink = mixed[0:count // 2 * 2:2], mixed[1:count // 2 * 2:2]
    slack = jnp.minimum(tallies[giver] - 1, limit - tallies[sink]) // 2
    slack = jnp.where((giver == order[0]) | (sink == order[0]) | (tallies[sink] == 0), 0, jnp.maximum(slack, 0))
    shifted = jax.random.randint(jax.random.fold_in(own, 4), (count // 2,), 0, 1 << 20) % (slack + 1)
    tallies = tallies.at[giver].add(-shifted).at[sink].add(shifted)
    labels = jnp.searchsorted(jnp.cumsum(tallies), jnp.arange(rows * top), side="right").astype(jnp.int32)
    table = labels.reshape(top, rows).T
    table = table[jax.random.permutation(jax.random.fold_in(own, 1), rows)]
    offset_by = jax.random.randint(jax.random.fold_in(own, 2), (rows, 1), 0, top)
    return jnp.take_along_axis(table, (jnp.arange(top)[None, :] + offset_by) % top, axis=1)


def load_shares(number_of, total, reach, slope, full):
    weights = [(1 << 20) // math.isqrt(standing ** slope) + 1 for standing in range(1, number_of + 1)]
    largest = reach if full else min(reach, max(-(-total // number_of), total * weights[0] // sum(weights)))
    least = 1 if total - largest >= number_of - 1 else 0
    counts, rest = [largest] + [least] * (number_of - 1), total - largest - least * (number_of - 1)
    while rest > 0:
        movable = [i for i in range(1, number_of) if counts[i] < largest] or [i for i in range(1, number_of) if counts[i] < reach]
        mass, budget = sum([weights[i] for i in movable]), rest
        for i in movable:
            addition = min(reach - counts[i], max(1, budget * weights[i] // mass), rest)
            counts[i] = counts[i] + addition
            rest = rest - addition
    return np.array(counts)


def centred(rng, shape, scale, limit, cuts=(), kind=jnp.bfloat16):
    values = scale * jax.random.normal(rng, shape, jnp.float32)
    if cuts:
        values = values * level_of(rng, shape, cuts, -0.22, 0.18)
    return jnp.clip(values, -limit, limit).astype(kind)


def setup_inputs(seed: int = 0) -> dict:
    key_list = jax.random.split(jax.random.key(seed), 7)
    records = centred(key_list[0], (STATIONS, 3, DLEN), 1.0, 6.0, ((0, 32),))
    templates = centred(key_list[1], (TEMPLATES, PICKS, 3, TLEN), 1.0, 6.0, ((0, 32),))
    pick_owner_keys = jax.random.split(jax.random.fold_in(key_list[2], 1), TEMPLATES // TPL_LOC)
    pick_owner_turns = jax.random.permutation(jax.random.fold_in(key_list[2], 3), TEMPLATES // TPL_LOC)
    pick_owner = jax.vmap(lambda own, number: routed_block(jax.random.fold_in(key_list[2], 2), own, number, TPL_LOC, DEVICES, PICKS, CAP, 2))(pick_owner_keys, pick_owner_turns).reshape((TEMPLATES, PICKS))
    pick_local = set_ends(jax.random.randint(key_list[3], (TEMPLATES, PICKS), 0, STA_LOC), jax.random.fold_in(key_list[3], 1), 0, STA_LOC - 1).astype(jnp.int32)
    moveout = set_ends(jax.random.randint(key_list[4], (TEMPLATES, PICKS), 0, 128), jax.random.fold_in(key_list[4], 1), 0, 127).astype(jnp.int32)
    channel_mask = set_ends((jax.random.randint(key_list[5], (TEMPLATES, PICKS, 3), 0, 5) < 4).astype(jnp.int32), jax.random.fold_in(key_list[5], 1), 0, 1)
    return dict(records=records, templates=templates, pick_owner=pick_owner, pick_local=pick_local, moveout=moveout, channel_mask=channel_mask)


EPS = 1e-06

def reference(records, templates, pick_owner, pick_local, moveout, channel_mask):
    lag_span = LAGS + 128
    length = 2 ** int(math.ceil(math.log2(DLEN)))
    signal = records.astype(jnp.float32)
    spectra = jnp.fft.rfft(signal, n=length, axis=-1)
    energy = lax.reduce_window(signal * signal, jnp.zeros((), jnp.float32), lax.add, (1, 1, TLEN), (1, 1, 1), 'VALID')[:, :, :lag_span]
    station = pick_owner * STA_LOC + pick_local
    block_size = math.gcd(TEMPLATES, 64)
    block_total = TEMPLATES // block_size

    def per_block(pieces):
        shapes, stations, mask_rows, shifts = pieces
        shapes = shapes.astype(jnp.float32)
        template_spec = jnp.fft.rfft(shapes, n=length, axis=-1)
        correlated = jnp.fft.irfft(jnp.conj(template_spec) * spectra[stations], n=length, axis=-1)[..., :lag_span]
        template_power = lax.optimization_barrier(jnp.sum(shapes * shapes, axis=-1))[..., None]
        scaled = correlated * lax.rsqrt(template_power * energy[stations] + EPS)
        traces = lax.optimization_barrier(jnp.sum(mask_rows.astype(jnp.float32)[..., None] * scaled, axis=2)).astype(jnp.bfloat16)
        indices = shifts[..., None] + jnp.arange(LAGS, dtype=jnp.int32)[None, None, :]
        aligned = jnp.take_along_axis(traces, indices, axis=-1).astype(jnp.float32)
        stacked = lax.optimization_barrier(jnp.sum(aligned, axis=1))
        levels = jnp.sqrt(lax.optimization_barrier(jnp.mean(stacked * stacked, axis=-1, keepdims=True)) + EPS)
        return stacked / levels
    result = lax.map(per_block, (templates.reshape(block_total, block_size, PICKS, 3, TLEN), station.reshape(block_total, block_size, PICKS), channel_mask.reshape(block_total, block_size, PICKS, 3), moveout.reshape(block_total, block_size, PICKS)))
    return result.reshape(TEMPLATES, LAGS)
```

```python
import functools

import jax
import jax.numpy as jnp
from jax import lax
from jax.experimental import pallas as pl
from jax.experimental.pallas import tpu as pltpu
from jax.sharding import PartitionSpec as P

EPS = 1e-06
LANES = 128


def toeplitz(row):
    base = pltpu.roll(
        jnp.broadcast_to(row, (16, 256)), 0, axis=1, stride=1, stride_axis=0
    ).astype(jnp.bfloat16)
    zeros = jnp.zeros((16, LANES), jnp.bfloat16)
    wide = jnp.concatenate([base, zeros], axis=1)
    strips = [wide]
    for step in range(1, 8):
        strips.append(
            jnp.concatenate([zeros[:, : 16 * step], wide[:, : 384 - 16 * step]], axis=1)
        )
    return jnp.concatenate(strips, axis=0)


def stack_kernel(picks, channels, blocks, station, shift, power, mask, band_ref, shapes_ref, *rest):
    record_refs, out_ref, wide_ref, squares_ref, energy_ref = rest[:picks], *rest[picks:]
    pieces = record_refs[0].shape[1] // channels
    rows = squares_ref.shape[0] // (picks * channels)
    template = pl.program_id(0)
    shapes = shapes_ref[0].astype(jnp.float32)
    for pick in range(picks):
        wide_ref[pick, : channels * pieces] = record_refs[pick][0].astype(jnp.float32)
    windows = []
    for pick in range(picks):
        for channel in range(channels):
            parts = [
                wide_ref[pick, channel * pieces + k : channel * pieces + k + rows]
                for k in range(3)
            ]
            windows.append(jnp.concatenate([part.astype(jnp.bfloat16) for part in parts], axis=1))
            item = pick * channels + channel
            squares_ref[item * rows : (item + 1) * rows] = jnp.concatenate(
                [(part * part).astype(jnp.bfloat16) for part in parts], axis=1
            )
    energy_ref[...] = jnp.dot(
        squares_ref[...], band_ref[...], preferred_element_type=jnp.float32
    )
    lane = lax.broadcasted_iota(jnp.int32, (blocks, LANES), 1)
    total = jnp.zeros((blocks, LANES), jnp.float32)
    for pick in range(picks):
        trace = jnp.zeros((rows, LANES), jnp.float32)
        for channel in range(channels):
            item = pick * channels + channel
            at = template * (picks * channels) + item
            correlation = lax.dot_general(
                windows[item],
                toeplitz(shapes[item : item + 1]),
                (((1,), (1,)), ((), ())),
                preferred_element_type=jnp.float32,
            )
            scale = lax.rsqrt(power[at] * energy_ref[item * rows : (item + 1) * rows] + EPS)
            trace = trace + mask[at] * (correlation * scale)
        trace = trace.astype(jnp.bfloat16).astype(jnp.float32)
        moved = shift[template * picks + pick]
        turned = pltpu.roll(trace, lax.rem(LANES - moved, LANES), axis=1)
        total = total + jnp.where(
            lane < LANES - moved, turned[:blocks], turned[1 : blocks + 1]
        )
    mean = jnp.sum(total * total) / (blocks * LANES)
    out_ref[0] = total * lax.rsqrt(jnp.full((blocks, LANES), mean + EPS, jnp.float32))


def on_device(records, templates, pick_owner, pick_local, moveout, channel_mask):
    own_stations, channels, record_len = records.shape
    own_templates, picks, _, shape_len = templates.shape
    pieces = record_len // LANES
    frame_len = 3 * LANES
    blocks = (record_len - frame_len) // LANES
    rows = -(-(blocks + 1) // 8) * 8
    everywhere = lax.all_gather(
        records.reshape(own_stations, channels * pieces, LANES), ("sta", "tpl"), axis=0, tiled=True
    )
    station = (pick_owner * own_stations + pick_local).reshape(-1)
    power = jnp.sum(jnp.square(templates.astype(jnp.float32)), axis=3).reshape(-1)
    mask = channel_mask.astype(jnp.float32).reshape(-1)
    items = picks * channels
    shapes = jnp.pad(
        templates.reshape(own_templates, items, shape_len),
        ((0, 0), (0, -items % 16), (0, 2 * LANES - shape_len)),
    )
    offsets = (
        jnp.arange(frame_len, dtype=jnp.int32)[:, None] - jnp.arange(LANES, dtype=jnp.int32)[None, :]
    )
    band = ((offsets >= 0) & (offsets < shape_len)).astype(jnp.bfloat16)

    def record_spec(pick):
        return pl.BlockSpec(
            (1, channels * pieces, LANES),
            lambda t, station, shift, power, mask: (station[t * picks + pick], 0, 0),
        )

    wide_rows = -(-((channels - 1) * pieces + 2 + rows) // 8) * 8
    stacked = pl.pallas_call(
        functools.partial(stack_kernel, picks, channels, blocks),
        grid_spec=pltpu.PrefetchScalarGridSpec(
            num_scalar_prefetch=4,
            grid=(own_templates,),
            in_specs=[
                pl.BlockSpec((frame_len, LANES), lambda t, *_: (0, 0)),
                pl.BlockSpec((1,) + shapes.shape[1:], lambda t, *_: (t, 0, 0)),
            ]
            + [record_spec(pick) for pick in range(picks)],
            out_specs=pl.BlockSpec((1, blocks, LANES), lambda t, *_: (t, 0, 0)),
            scratch_shapes=[
                pltpu.VMEM((picks, wide_rows, LANES), jnp.float32),
                pltpu.VMEM((items * rows, frame_len), jnp.bfloat16),
                pltpu.VMEM((items * rows, LANES), jnp.float32),
            ],
        ),
        out_shape=jax.ShapeDtypeStruct((own_templates, blocks, LANES), jnp.float32),
        compiler_params=pltpu.CompilerParams(vmem_limit_bytes=48 * 1024 * 1024),
    )(station, moveout.reshape(-1), power, mask, band, shapes, *([everywhere] * picks))
    return stacked.reshape(own_templates, blocks * LANES)


def solution(mesh):
    return jax.shard_map(
        on_device,
        mesh=mesh,
        in_specs=(
            P(("sta", "tpl"), None, None),
            P(("sta", "tpl"), None, None, None),
            P(("sta", "tpl"), None),
            P(("sta", "tpl"), None),
            P(("sta", "tpl"), None),
            P(("sta", "tpl"), None, None),
        ),
        out_specs=P(("sta", "tpl"), None),
        check_vma=False,
    )
```

```python
import functools

import jax
import jax.numpy as jnp
from jax import lax
from jax.experimental import pallas as pl
from jax.experimental.pallas import tpu as pltpu
from jax.sharding import PartitionSpec as P

EPS = 1e-06
LANES = 128
MESH = pl.DeviceIdType.MESH


def toeplitz(row):
    base = pltpu.roll(
        jnp.broadcast_to(row, (16, 256)), 0, axis=1, stride=1, stride_axis=0
    ).astype(jnp.bfloat16)
    zeros = jnp.zeros((16, LANES), jnp.bfloat16)
    wide = jnp.concatenate([base, zeros], axis=1)
    strips = [wide]
    for step in range(1, 8):
        strips.append(
            jnp.concatenate([zeros[:, : 16 * step], wide[:, : 384 - 16 * step]], axis=1)
        )
    return jnp.concatenate(strips, axis=0)


def stack_kernel(picks, channels, pieces, station, shift, power, mask, band_ref, shapes_ref, *rest):
    record_refs, out_ref, wide_ref, squares_ref, energy_ref = rest[:picks], *rest[picks:]
    blocks = out_ref.shape[1]
    held = record_refs[0].shape[1]
    template = pl.program_id(0)
    shapes = shapes_ref[0].astype(jnp.float32)
    lane = lax.broadcasted_iota(jnp.int32, (held, LANES), 1)
    windows = []
    for pick in range(picks):
        moved = shift[template * picks + pick]
        wide_ref[pick, :held] = pltpu.roll(
            record_refs[pick][0].astype(jnp.float32), lax.rem(LANES - moved, LANES), axis=1
        )
        wide_ref[pick, :held] = jnp.where(
            lane < LANES - moved, wide_ref[pick, :held], wide_ref[pick, 1 : held + 1]
        )
        for channel in range(channels):
            first = channel * pieces
            window = jnp.concatenate(
                [
                    wide_ref[pick, first + k : first + k + blocks].astype(jnp.bfloat16)
                    for k in range(3)
                ],
                axis=1,
            )
            windows.append(window)
            item = pick * channels + channel
            squares_ref[item * blocks : (item + 1) * blocks] = window * window
    energy_ref[...] = jnp.dot(
        squares_ref[...], band_ref[...], preferred_element_type=jnp.float32
    )
    total = jnp.zeros((blocks, LANES), jnp.float32)
    for pick in range(picks):
        trace = jnp.zeros((blocks, LANES), jnp.float32)
        for channel in range(channels):
            item = pick * channels + channel
            at = template * (picks * channels) + item
            correlation = lax.dot_general(
                windows[item],
                toeplitz(shapes[item : item + 1]),
                (((1,), (1,)), ((), ())),
                preferred_element_type=jnp.float32,
            )
            scale = lax.rsqrt(power[at] * energy_ref[item * blocks : (item + 1) * blocks] + EPS)
            trace = trace + mask[at] * (correlation * scale)
        total = total + trace.astype(jnp.bfloat16).astype(jnp.float32)
    mean = jnp.sum(total * total) / (blocks * LANES)
    out_ref[0] = total * lax.rsqrt(jnp.full((blocks, LANES), mean + EPS, jnp.float32))


def gather_kernel(mine_ref, all_ref, local_sem, send_sem, recv_sem):
    stations = mine_ref.shape[0]
    sta, tpl = lax.axis_index("sta"), lax.axis_index("tpl")
    z, x, y, core = sta // 2, sta % 2, tpl // 2, tpl % 2
    first_x, first_y = x + (1 - core) * (1 - 2 * x), y + core * (1 - 2 * y)
    second_x, second_y = x + core * (1 - 2 * x), y + (1 - core) * (1 - 2 * y)
    heights = [z, z + 1 - 2 * (z % 2), (z + 2) % 4, 3 - z]
    first = (z * 2 + first_x, first_y * 2 + core)
    second = (z * 2 + second_x, second_y * 2 + core)
    sibling = (sta, y * 2 + 1 - core)
    partners = [(height * 2 + x, tpl) for height in heights[1:]] + [first, second, sibling]

    barrier = pltpu.get_barrier_semaphore()
    for partner in partners:
        pl.semaphore_signal(barrier, inc=1, device_id=partner, device_id_type=MESH)
    pl.semaphore_wait(barrier, len(partners))

    def number(height, at_x, at_y, at_core):
        return (height * 2 + at_x) * 4 + at_y * 2 + at_core

    def block(shard):
        return all_ref.at[pl.ds(shard * stations, stations)]

    started = []

    def send(source, shard, partner):
        copy = pltpu.make_async_remote_copy(
            src_ref=source,
            dst_ref=block(shard),
            send_sem=send_sem.at[len(started)],
            recv_sem=recv_sem.at[shard],
            device_id=partner,
            device_id_type=MESH,
        )
        copy.start()
        started.append(copy)

    def arrive(shard):
        pltpu.make_async_remote_copy(
            src_ref=block(shard),
            dst_ref=block(shard),
            send_sem=send_sem.at[0],
            recv_sem=recv_sem.at[shard],
            device_id=sibling,
            device_id_type=MESH,
        ).wait_recv()

    own = number(z, x, y, core)
    for partner in partners:
        send(mine_ref, own, partner)
    local = pltpu.make_async_copy(mine_ref, block(own), local_sem)
    local.start()

    def far(height):
        for at_x, at_y in ((second_x, second_y), (1 - x, 1 - y)):
            shard = number(height, at_x, at_y, core)
            arrive(shard)
            send(block(shard), shard, sibling)

    for step, height in enumerate(heights):
        if step:
            shard = number(height, x, y, core)
            arrive(shard)
            for partner in (first, second, sibling):
                send(block(shard), shard, partner)
        shard = number(height, first_x, first_y, core)
        arrive(shard)
        for partner in (second, sibling):
            send(block(shard), shard, partner)
        if step:
            far(heights[step - 1])
    far(heights[-1])
    for height in heights:
        for at_x, at_y in ((x, y), (first_x, first_y), (second_x, second_y), (1 - x, 1 - y)):
            arrive(number(height, at_x, at_y, 1 - core))
    local.wait()
    for copy in started:
        copy.wait_send()


def gathered(block):
    devices = lax.axis_size(("sta", "tpl"))
    if (lax.axis_size("sta"), lax.axis_size("tpl")) != (8, 4):
        return lax.all_gather(block, ("sta", "tpl"), axis=0, tiled=True)
    return pl.pallas_call(
        gather_kernel,
        in_specs=[pl.BlockSpec(memory_space=pl.ANY)],
        out_specs=pl.BlockSpec(memory_space=pl.ANY),
        out_shape=jax.ShapeDtypeStruct((devices * block.shape[0],) + block.shape[1:], block.dtype),
        scratch_shapes=[
            pltpu.SemaphoreType.DMA,
            pltpu.SemaphoreType.DMA((devices - 1,)),
            pltpu.SemaphoreType.DMA((devices,)),
        ],
        compiler_params=pltpu.CompilerParams(collective_id=0, has_side_effects=True),
    )(block)


def on_device(records, templates, pick_owner, pick_local, moveout, channel_mask):
    own_stations, channels, record_len = records.shape
    own_templates, picks, _, shape_len = templates.shape
    pieces = record_len // LANES
    frame_len = 3 * LANES
    blocks = (record_len - frame_len) // LANES
    held = -(-channels * pieces // 16) * 16
    everywhere = gathered(
        jnp.pad(
            records.reshape(own_stations, channels * pieces, LANES),
            ((0, 0), (0, held - channels * pieces), (0, 0)),
        )
    )
    station = (pick_owner * own_stations + pick_local).reshape(-1)
    power = jnp.sum(jnp.square(templates.astype(jnp.float32)), axis=3).reshape(-1)
    mask = channel_mask.astype(jnp.float32).reshape(-1)
    items = picks * channels
    shapes = jnp.pad(
        templates.reshape(own_templates, items, shape_len),
        ((0, 0), (0, -items % 16), (0, 2 * LANES - shape_len)),
    )
    offsets = (
        jnp.arange(frame_len, dtype=jnp.int32)[:, None] - jnp.arange(LANES, dtype=jnp.int32)[None, :]
    )
    band = ((offsets >= 0) & (offsets < shape_len)).astype(jnp.bfloat16)

    def record_spec(pick):
        return pl.BlockSpec(
            (1, held, LANES),
            lambda t, station, shift, power, mask: (station[t * picks + pick], 0, 0),
        )

    stacked = pl.pallas_call(
        functools.partial(stack_kernel, picks, channels, pieces),
        grid_spec=pltpu.PrefetchScalarGridSpec(
            num_scalar_prefetch=4,
            grid=(own_templates,),
            in_specs=[
                pl.BlockSpec((frame_len, LANES), lambda t, *_: (0, 0)),
                pl.BlockSpec((1,) + shapes.shape[1:], lambda t, *_: (t, 0, 0)),
            ]
            + [record_spec(pick) for pick in range(picks)],
            out_specs=pl.BlockSpec((1, blocks, LANES), lambda t, *_: (t, 0, 0)),
            scratch_shapes=[
                pltpu.VMEM((picks, held + 8, LANES), jnp.float32),
                pltpu.VMEM((items * blocks, frame_len), jnp.bfloat16),
                pltpu.VMEM((items * blocks, LANES), jnp.float32),
            ],
        ),
        out_shape=jax.ShapeDtypeStruct((own_templates, blocks, LANES), jnp.float32),
        compiler_params=pltpu.CompilerParams(vmem_limit_bytes=48 * 1024 * 1024),
    )(station, moveout.reshape(-1), power, mask, band, shapes, *([everywhere] * picks))
    return stacked.reshape(own_templates, blocks * LANES)


def solution(mesh):
    return jax.shard_map(
        on_device,
        mesh=mesh,
        in_specs=(
            P(("sta", "tpl"), None, None),
            P(("sta", "tpl"), None, None, None),
            P(("sta", "tpl"), None),
            P(("sta", "tpl"), None),
            P(("sta", "tpl"), None),
            P(("sta", "tpl"), None, None),
        ),
        out_specs=P(("sta", "tpl"), None),
        check_vma=False,
    )
```

```python
import functools

import jax
import jax.numpy as jnp
from jax import lax
from jax.experimental import pallas as pl
from jax.experimental.pallas import tpu as pltpu
from jax.sharding import PartitionSpec as P

EPS = 1e-06
LANES = 128
MESH = pl.DeviceIdType.MESH


def toeplitz(row):
    base = pltpu.roll(
        jnp.broadcast_to(row, (16, 256)), 0, axis=1, stride=1, stride_axis=0
    ).astype(jnp.bfloat16)
    zeros = jnp.zeros((16, LANES), jnp.bfloat16)
    wide = jnp.concatenate([base, zeros], axis=1)
    strips = [wide]
    for step in range(1, 8):
        strips.append(
            jnp.concatenate([zeros[:, : 16 * step], wide[:, : 384 - 16 * step]], axis=1)
        )
    return jnp.concatenate(strips, axis=0)


def stack_kernel(picks, channels, pieces, station, shift, power, mask, band_ref, shapes_ref, *rest):
    record_refs, out_ref, wide_ref, squares_ref, energy_ref = rest[:picks], *rest[picks:]
    blocks = out_ref.shape[1]
    held = record_refs[0].shape[1]
    template = pl.program_id(0)
    shapes = shapes_ref[0].astype(jnp.float32)
    lane = lax.broadcasted_iota(jnp.int32, (held, LANES), 1)
    windows = []
    for pick in range(picks):
        moved = shift[template * picks + pick]
        wide_ref[pick, :held] = pltpu.roll(
            record_refs[pick][0].astype(jnp.float32), lax.rem(LANES - moved, LANES), axis=1
        )
        wide_ref[pick, :held] = jnp.where(
            lane < LANES - moved, wide_ref[pick, :held], wide_ref[pick, 1 : held + 1]
        )
        for channel in range(channels):
            first = channel * pieces
            window = jnp.concatenate(
                [
                    wide_ref[pick, first + k : first + k + blocks].astype(jnp.bfloat16)
                    for k in range(3)
                ],
                axis=1,
            )
            windows.append(window)
            item = pick * channels + channel
            squares_ref[item * blocks : (item + 1) * blocks] = window * window
    energy_ref[...] = jnp.dot(
        squares_ref[...], band_ref[...], preferred_element_type=jnp.float32
    )
    total = jnp.zeros((blocks, LANES), jnp.float32)
    for pick in range(picks):
        trace = jnp.zeros((blocks, LANES), jnp.float32)
        for channel in range(channels):
            item = pick * channels + channel
            at = template * (picks * channels) + item
            correlation = lax.dot_general(
                windows[item],
                toeplitz(shapes[item : item + 1]),
                (((1,), (1,)), ((), ())),
                preferred_element_type=jnp.float32,
            )
            scale = lax.rsqrt(power[at] * energy_ref[item * blocks : (item + 1) * blocks] + EPS)
            trace = trace + mask[at] * (correlation * scale)
        total = total + trace.astype(jnp.bfloat16).astype(jnp.float32)
    mean = jnp.sum(total * total) / (blocks * LANES)
    out_ref[0] = total * lax.rsqrt(jnp.full((blocks, LANES), mean + EPS, jnp.float32))


def fused_kernel(
    picks, channels, pieces, base, shift, power, mask, band_ref, shapes_ref, mine_ref, out_ref, *scratch
):
    landed = scratch[:channels]
    wide_ref, turned_ref, squares_ref, energy_ref, traces_ref, local_sem, send_sem, recv_sem = scratch[channels:]
    templates, blocks = out_ref.shape[0], out_ref.shape[1]
    devices, block_rows = landed[0].shape[0], landed[0].shape[1]
    sta, tpl = lax.axis_index("sta"), lax.axis_index("tpl")
    z, x, y, core = sta // 2, sta % 2, tpl // 2, tpl % 2
    first_x, first_y = x + (1 - core) * (1 - 2 * x), y + core * (1 - 2 * y)
    second_x, second_y = x + core * (1 - 2 * x), y + (1 - core) * (1 - 2 * y)
    heights = [z, z + 1 - 2 * (z % 2), (z + 2) % 4, 3 - z]
    first = (z * 2 + first_x, first_y * 2 + core)
    second = (z * 2 + second_x, second_y * 2 + core)
    sibling = (sta, y * 2 + 1 - core)
    partners = [(height * 2 + x, tpl) for height in heights[1:]] + [first, second, sibling]

    def number(height, at_x, at_y, at_core):
        return (height * 2 + at_x) * 4 + at_y * 2 + at_core

    own = number(z, x, y, core)
    plan = [[(None, own, partner) for partner in partners]]
    for step, height in enumerate(heights):
        moves = []
        shard = number(height, x, y, core)
        if step:
            moves += [(shard, None, None)]
            moves += [(None, shard, partner) for partner in (first, second, sibling)]
        shard = number(height, first_x, first_y, core)
        moves += [(shard, None, None)]
        moves += [(None, shard, partner) for partner in (second, sibling)]
        plan.append(moves)
    for step, height in enumerate(heights):
        moves = plan[min(step + 2, 4)] if step < 3 else []
        for at_x, at_y in ((second_x, second_y), (1 - x, 1 - y)):
            shard = number(height, at_x, at_y, core)
            moves += [(shard, None, None), (None, shard, sibling)]
        if step == 3:
            plan.append(moves)
    last = []
    for height in heights:
        for at_x, at_y in ((x, y), (first_x, first_y), (second_x, second_y), (1 - x, 1 - y)):
            last.append((number(height, at_x, at_y, 1 - core), None, None))
    plan.append(last)
    firsts = [sum(move[0] is None for moves in plan[:k] for move in moves) for k in range(len(plan))]

    def copy_of(channel, index, shard, partner, source=None):
        place = landed[channel].at[shard]
        return pltpu.make_async_remote_copy(
            src_ref=place if source is None else source,
            dst_ref=place,
            send_sem=send_sem.at[channel, index],
            recv_sem=recv_sem.at[channel, shard],
            device_id=partner,
            device_id_type=MESH,
        )

    def run(channel, part):
        index = firsts[part]
        for arrival, shard, partner in plan[part]:
            if arrival is not None:
                copy_of(channel, 0, arrival, sibling).wait_recv()
            else:
                copy_of(
                    channel, index, shard, partner, mine_ref.at[channel] if part == 0 else None
                ).start()
                index += 1

    def local(channel):
        return pltpu.make_async_copy(
            mine_ref.at[channel], landed[channel].at[own], local_sem.at[channel]
        )

    barrier = pltpu.get_barrier_semaphore()
    for partner in partners:
        pl.semaphore_signal(barrier, inc=1, device_id=partner, device_id_type=MESH)
    pl.semaphore_wait(barrier, len(partners))
    for channel in range(channels):
        local(channel).start()
    run(0, 0)
    for part in (1, 2):
        run(0, part)
    run(1, 0)
    for part in (3, 4, 5):
        run(0, part)

    lane = lax.broadcasted_iota(jnp.int32, (blocks, LANES), 1)
    for channel in range(channels):
        run(channel, 6)
        local(channel).wait()

        def widen(device, carry, channel=channel):
            at = pl.multiple_of(device * block_rows, 16)
            wide_ref[pl.ds(at, block_rows)] = landed[channel][device].astype(jnp.float32)
            return carry

        lax.fori_loop(0, devices, widen, 0)

        def stack(template, carry, channel=channel):
            if channel + 1 < channels:
                for part in range(1, 6):

                    @pl.when(template == 4 * part - 3)
                    def _(part=part):
                        run(channel + 1, part)

            if channel + 2 < channels:

                @pl.when(template == 10)
                def _():
                    run(channel + 2, 0)

            shapes = shapes_ref[channel, template].astype(jnp.float32)
            windows = []
            for pick in range(picks):
                item = template * picks + pick
                moved = shift[item]
                turned_ref[pick] = pltpu.roll(
                    wide_ref[pl.ds(base[item], turned_ref.shape[1])],
                    lax.rem(LANES - moved, LANES),
                    axis=1,
                )
                window = jnp.concatenate(
                    [
                        jnp.where(
                            lane < LANES - moved,
                            turned_ref[pick, k : k + blocks],
                            turned_ref[pick, k + 1 : k + 1 + blocks],
                        ).astype(jnp.bfloat16)
                        for k in range(3)
                    ],
                    axis=1,
                )
                windows.append(window)
                squares_ref[pick * blocks : (pick + 1) * blocks] = window * window
            energy_ref[...] = jnp.dot(
                squares_ref[...], band_ref[...], preferred_element_type=jnp.float32
            )
            total = jnp.zeros((blocks, LANES), jnp.float32)
            for pick in range(picks):
                item = template * picks + pick
                correlation = lax.dot_general(
                    windows[pick],
                    toeplitz(shapes[pick : pick + 1]),
                    (((1,), (1,)), ((), ())),
                    preferred_element_type=jnp.float32,
                )
                at = item * channels + channel
                scale = lax.rsqrt(
                    power[at] * energy_ref[pick * blocks : (pick + 1) * blocks] + EPS
                )
                trace = mask[at] * (correlation * scale)
                if channel:
                    trace = trace + traces_ref[item]
                if channel + 1 < channels:
                    traces_ref[item] = trace
                else:
                    total = total + trace.astype(jnp.bfloat16).astype(jnp.float32)
            if channel + 1 == channels:
                mean = jnp.sum(total * total) / (blocks * LANES)
                out_ref[template] = total * lax.rsqrt(
                    jnp.full((blocks, LANES), mean + EPS, jnp.float32)
                )
            return carry

        lax.fori_loop(0, templates, stack, 0)
    for channel in range(channels):
        index = 0
        for part, moves in enumerate(plan):
            for arrival, shard, partner in moves:
                if arrival is None:
                    copy_of(
                        channel, index, shard, partner, mine_ref.at[channel] if part == 0 else None
                    ).wait_send()
                    index += 1


def fused(records, templates, pick_owner, pick_local, moveout, power, mask, band):
    devices = lax.axis_size(("sta", "tpl"))
    own_stations, channels, record_len = records.shape
    own_templates, picks, _, shape_len = templates.shape
    pieces = record_len // LANES
    blocks = record_len // LANES - 3
    block_rows = -(-own_stations * pieces // 16) * 16
    mine = jnp.pad(
        jnp.transpose(records.reshape(own_stations, channels, pieces, LANES), (1, 0, 2, 3)).reshape(
            channels, own_stations * pieces, LANES
        ),
        ((0, 0), (0, block_rows - own_stations * pieces), (0, 0)),
    )
    shapes = jnp.pad(
        jnp.transpose(templates, (2, 0, 1, 3)),
        ((0, 0), (0, 0), (0, -picks % 16), (0, 2 * LANES - shape_len)),
    )
    base = (pick_owner * block_rows + pick_local * pieces).reshape(-1)
    smem = pl.BlockSpec(memory_space=pltpu.SMEM)
    vmem = pl.BlockSpec(memory_space=pltpu.VMEM)
    return pl.pallas_call(
        functools.partial(fused_kernel, picks, channels, pieces),
        in_specs=[smem] * 4 + [vmem] * 2 + [pl.BlockSpec(memory_space=pl.ANY)],
        out_specs=vmem,
        out_shape=jax.ShapeDtypeStruct((own_templates, blocks, LANES), jnp.float32),
        scratch_shapes=[pltpu.VMEM((devices, block_rows, LANES), jnp.bfloat16)] * channels
        + [
            pltpu.VMEM((devices * block_rows, LANES), jnp.float32),
            pltpu.VMEM((picks, blocks + 8, LANES), jnp.float32),
            pltpu.VMEM((picks * blocks, 3 * LANES), jnp.bfloat16),
            pltpu.VMEM((picks * blocks, LANES), jnp.float32),
            pltpu.VMEM((own_templates * picks, blocks, LANES), jnp.float32),
            pltpu.SemaphoreType.DMA((channels,)),
            pltpu.SemaphoreType.DMA((channels, devices - 1)),
            pltpu.SemaphoreType.DMA((channels, devices)),
        ],
        compiler_params=pltpu.CompilerParams(
            collective_id=0, has_side_effects=True, vmem_limit_bytes=48 * 1024 * 1024
        ),
    )(base, moveout.reshape(-1), power, mask, band, shapes, mine)


def on_device(records, templates, pick_owner, pick_local, moveout, channel_mask):
    own_stations, channels, record_len = records.shape
    own_templates, picks, _, shape_len = templates.shape
    pieces = record_len // LANES
    frame_len = 3 * LANES
    blocks = (record_len - frame_len) // LANES
    power = jnp.sum(jnp.square(templates.astype(jnp.float32)), axis=3).reshape(-1)
    mask = channel_mask.astype(jnp.float32).reshape(-1)
    offsets = (
        jnp.arange(frame_len, dtype=jnp.int32)[:, None] - jnp.arange(LANES, dtype=jnp.int32)[None, :]
    )
    band = ((offsets >= 0) & (offsets < shape_len)).astype(jnp.bfloat16)

    if (lax.axis_size("sta"), lax.axis_size("tpl"), channels) == (8, 4, 3):
        stacked = fused(records, templates, pick_owner, pick_local, moveout, power, mask, band)
        return stacked.reshape(own_templates, blocks * LANES)

    held = -(-channels * pieces // 16) * 16
    everywhere = lax.all_gather(
        jnp.pad(
            records.reshape(own_stations, channels * pieces, LANES),
            ((0, 0), (0, held - channels * pieces), (0, 0)),
        ),
        ("sta", "tpl"),
        axis=0,
        tiled=True,
    )
    station = (pick_owner * own_stations + pick_local).reshape(-1)
    items = picks * channels
    shapes = jnp.pad(
        templates.reshape(own_templates, items, shape_len),
        ((0, 0), (0, -items % 16), (0, 2 * LANES - shape_len)),
    )

    def record_spec(pick):
        return pl.BlockSpec(
            (1, held, LANES),
            lambda t, station, shift, power, mask: (station[t * picks + pick], 0, 0),
        )

    stacked = pl.pallas_call(
        functools.partial(stack_kernel, picks, channels, pieces),
        grid_spec=pltpu.PrefetchScalarGridSpec(
            num_scalar_prefetch=4,
            grid=(own_templates,),
            in_specs=[
                pl.BlockSpec((frame_len, LANES), lambda t, *_: (0, 0)),
                pl.BlockSpec((1,) + shapes.shape[1:], lambda t, *_: (t, 0, 0)),
            ]
            + [record_spec(pick) for pick in range(picks)],
            out_specs=pl.BlockSpec((1, blocks, LANES), lambda t, *_: (t, 0, 0)),
            scratch_shapes=[
                pltpu.VMEM((picks, held + 8, LANES), jnp.float32),
                pltpu.VMEM((items * blocks, frame_len), jnp.bfloat16),
                pltpu.VMEM((items * blocks, LANES), jnp.float32),
            ],
        ),
        out_shape=jax.ShapeDtypeStruct((own_templates, blocks, LANES), jnp.float32),
        compiler_params=pltpu.CompilerParams(vmem_limit_bytes=48 * 1024 * 1024),
    )(station, moveout.reshape(-1), power, mask, band, shapes, *([everywhere] * picks))
    return stacked.reshape(own_templates, blocks * LANES)


def solution(mesh):
    return jax.shard_map(
        on_device,
        mesh=mesh,
        in_specs=(
            P(("sta", "tpl"), None, None),
            P(("sta", "tpl"), None, None, None),
            P(("sta", "tpl"), None),
            P(("sta", "tpl"), None),
            P(("sta", "tpl"), None),
            P(("sta", "tpl"), None, None),
        ),
        out_specs=P(("sta", "tpl"), None),
        check_vma=False,
    )
```

```python
import functools

import jax
import jax.numpy as jnp
from jax import lax
from jax.experimental import pallas as pl
from jax.experimental.pallas import tpu as pltpu
from jax.sharding import PartitionSpec as P

EPS = 1e-06
LANES = 128
GROUP = 6
MESH = pl.DeviceIdType.MESH


def toeplitz(row):
    base = pltpu.roll(
        jnp.broadcast_to(row, (16, 256)), 0, axis=1, stride=1, stride_axis=0
    ).astype(jnp.bfloat16)
    zeros = jnp.zeros((16, LANES), jnp.bfloat16)
    wide = jnp.concatenate([base, zeros], axis=1)
    strips = [wide]
    for step in range(1, 8):
        strips.append(
            jnp.concatenate([zeros[:, : 16 * step], wide[:, : 384 - 16 * step]], axis=1)
        )
    return jnp.concatenate(strips, axis=0)


def stack_kernel(picks, channels, pieces, station, shift, power, mask, band_ref, shapes_ref, *rest):
    record_refs, out_ref, wide_ref, squares_ref, energy_ref = rest[:picks], *rest[picks:]
    blocks = out_ref.shape[1]
    held = record_refs[0].shape[1]
    template = pl.program_id(0)
    shapes = shapes_ref[0].astype(jnp.float32)
    lane = lax.broadcasted_iota(jnp.int32, (held, LANES), 1)
    windows = []
    for pick in range(picks):
        moved = shift[template * picks + pick]
        wide_ref[pick, :held] = pltpu.roll(
            record_refs[pick][0].astype(jnp.float32), lax.rem(LANES - moved, LANES), axis=1
        )
        wide_ref[pick, :held] = jnp.where(
            lane < LANES - moved, wide_ref[pick, :held], wide_ref[pick, 1 : held + 1]
        )
        for channel in range(channels):
            first = channel * pieces
            window = jnp.concatenate(
                [
                    wide_ref[pick, first + k : first + k + blocks].astype(jnp.bfloat16)
                    for k in range(3)
                ],
                axis=1,
            )
            windows.append(window)
            item = pick * channels + channel
            squares_ref[item * blocks : (item + 1) * blocks] = window * window
    energy_ref[...] = jnp.dot(
        squares_ref[...], band_ref[...], preferred_element_type=jnp.float32
    )
    total = jnp.zeros((blocks, LANES), jnp.float32)
    for pick in range(picks):
        trace = jnp.zeros((blocks, LANES), jnp.float32)
        for channel in range(channels):
            item = pick * channels + channel
            at = template * (picks * channels) + item
            correlation = lax.dot_general(
                windows[item],
                toeplitz(shapes[item : item + 1]),
                (((1,), (1,)), ((), ())),
                preferred_element_type=jnp.float32,
            )
            scale = lax.rsqrt(power[at] * energy_ref[item * blocks : (item + 1) * blocks] + EPS)
            trace = trace + mask[at] * (correlation * scale)
        total = total + trace.astype(jnp.bfloat16).astype(jnp.float32)
    mean = jnp.sum(total * total) / (blocks * LANES)
    out_ref[0] = total * lax.rsqrt(jnp.full((blocks, LANES), mean + EPS, jnp.float32))


def fused_kernel(
    picks, channels, pieces, base, shift, power, mask, band_ref, shapes_ref, mine_ref, out_ref, *scratch
):
    landed = scratch[:channels]
    wide_ref, turned_ref, windows_ref, energy_ref, traces_ref, local_sem, send_sem, recv_sem = scratch[channels:]
    templates, blocks = out_ref.shape[0], out_ref.shape[1]
    devices, block_rows = landed[0].shape[0], landed[0].shape[1]
    sta, tpl = lax.axis_index("sta"), lax.axis_index("tpl")
    z, x, y, core = sta // 2, sta % 2, tpl // 2, tpl % 2
    first_x, first_y = x + (1 - core) * (1 - 2 * x), y + core * (1 - 2 * y)
    second_x, second_y = x + core * (1 - 2 * x), y + (1 - core) * (1 - 2 * y)
    heights = [z, z + 1 - 2 * (z % 2), (z + 2) % 4, 3 - z]
    first = (z * 2 + first_x, first_y * 2 + core)
    second = (z * 2 + second_x, second_y * 2 + core)
    sibling = (sta, y * 2 + 1 - core)
    partners = [(height * 2 + x, tpl) for height in heights[1:]] + [first, second, sibling]

    def number(height, at_x, at_y, at_core):
        return (height * 2 + at_x) * 4 + at_y * 2 + at_core

    own = number(z, x, y, core)
    plan = [[(None, own, partner) for partner in partners]]
    for step, height in enumerate(heights):
        moves = []
        shard = number(height, x, y, core)
        if step:
            moves += [(shard, None, None)]
            moves += [(None, shard, partner) for partner in (first, second, sibling)]
        shard = number(height, first_x, first_y, core)
        moves += [(shard, None, None)]
        moves += [(None, shard, partner) for partner in (second, sibling)]
        plan.append(moves)
    for step, height in enumerate(heights):
        moves = plan[min(step + 2, 4)] if step < 3 else []
        for at_x, at_y in ((second_x, second_y), (1 - x, 1 - y)):
            shard = number(height, at_x, at_y, core)
            moves += [(shard, None, None), (None, shard, sibling)]
        if step == 3:
            plan.append(moves)
    last = []
    for height in heights:
        for at_x, at_y in ((x, y), (first_x, first_y), (second_x, second_y), (1 - x, 1 - y)):
            last.append((number(height, at_x, at_y, 1 - core), None, None))
    plan.append(last)
    firsts = [sum(move[0] is None for moves in plan[:k] for move in moves) for k in range(len(plan))]

    def copy_of(channel, index, shard, partner, source=None):
        place = landed[channel].at[shard]
        return pltpu.make_async_remote_copy(
            src_ref=place if source is None else source,
            dst_ref=place,
            send_sem=send_sem.at[channel, index],
            recv_sem=recv_sem.at[channel, shard],
            device_id=partner,
            device_id_type=MESH,
        )

    def run(channel, part):
        index = firsts[part]
        for arrival, shard, partner in plan[part]:
            if arrival is not None:
                copy_of(channel, 0, arrival, sibling).wait_recv()
            else:
                copy_of(
                    channel, index, shard, partner, mine_ref.at[channel] if part == 0 else None
                ).start()
                index += 1

    def local(channel):
        return pltpu.make_async_copy(
            mine_ref.at[channel], landed[channel].at[own], local_sem.at[channel]
        )

    barrier = pltpu.get_barrier_semaphore()
    for partner in partners:
        pl.semaphore_signal(barrier, inc=1, device_id=partner, device_id_type=MESH)
    pl.semaphore_wait(barrier, len(partners))
    for channel in range(channels):
        local(channel).start()
    run(0, 0)
    for part in (1, 2):
        run(0, part)
    run(1, 0)
    for part in (3, 4, 5):
        run(0, part)

    lane = lax.broadcasted_iota(jnp.int32, (blocks, LANES), 1)
    for channel in range(channels):
        run(channel, 6)
        local(channel).wait()

        def widen(device, carry, channel=channel):
            at = pl.multiple_of(device * block_rows, 16)
            wide_ref[pl.ds(at, block_rows)] = landed[channel][device].astype(jnp.float32)
            return carry

        lax.fori_loop(0, devices, widen, 0)

        def prepare(template, slot):
            for pick in range(picks):
                item = template * picks + pick
                moved = shift[item]
                turned_ref[slot, pick] = pltpu.roll(
                    wide_ref[pl.ds(base[item], turned_ref.shape[2])],
                    lax.rem(LANES - moved, LANES),
                    axis=1,
                )
                windows_ref[slot, pick * blocks : (pick + 1) * blocks] = jnp.concatenate(
                    [
                        jnp.where(
                            lane < LANES - moved,
                            turned_ref[slot, pick, k : k + blocks],
                            turned_ref[slot, pick, k + 1 : k + 1 + blocks],
                        ).astype(jnp.bfloat16)
                        for k in range(3)
                    ],
                    axis=1,
                )
            windows = windows_ref[slot]
            energy_ref[slot] = jnp.dot(
                windows * windows, band_ref[...], preferred_element_type=jnp.float32
            )

        def combine(template, slot, channel):
            shapes = shapes_ref[channel, template].astype(jnp.float32)
            total = jnp.zeros((blocks, LANES), jnp.float32)
            for pick in range(picks):
                item = template * picks + pick
                correlation = lax.dot_general(
                    windows_ref[slot, pick * blocks : (pick + 1) * blocks],
                    toeplitz(shapes[pick : pick + 1]),
                    (((1,), (1,)), ((), ())),
                    preferred_element_type=jnp.float32,
                )
                at = item * channels + channel
                scale = lax.rsqrt(
                    power[at] * energy_ref[slot, pick * blocks : (pick + 1) * blocks] + EPS
                )
                trace = mask[at] * (correlation * scale)
                if channel:
                    trace = trace + traces_ref[item]
                if channel + 1 < channels:
                    traces_ref[item] = trace
                else:
                    total = total + trace.astype(jnp.bfloat16).astype(jnp.float32)
            if channel + 1 == channels:
                mean = jnp.sum(total * total) / (blocks * LANES)
                out_ref[template] = total * lax.rsqrt(
                    jnp.full((blocks, LANES), mean + EPS, jnp.float32)
                )

        def stack(step, carry, channel=channel):
            if channel + 1 < channels:
                for at, parts in enumerate(((1,), (2, 3), (4,), (5,))):

                    @pl.when(step == at)
                    def _(parts=parts, at=at):
                        for part in parts:
                            run(channel + 1, part)
                        if channel + 2 < channels and at == 2:
                            run(channel + 2, 0)

            prepare(step * GROUP, 0)
            for slot in range(GROUP):
                if slot + 1 < GROUP:
                    prepare(step * GROUP + slot + 1, slot + 1)
                combine(step * GROUP + slot, slot, channel)
            return carry

        lax.fori_loop(0, templates // GROUP, stack, 0)
    for channel in range(channels):
        index = 0
        for part, moves in enumerate(plan):
            for arrival, shard, partner in moves:
                if arrival is None:
                    copy_of(
                        channel, index, shard, partner, mine_ref.at[channel] if part == 0 else None
                    ).wait_send()
                    index += 1


def fused(records, templates, pick_owner, pick_local, moveout, power, mask, band):
    devices = lax.axis_size(("sta", "tpl"))
    own_stations, channels, record_len = records.shape
    own_templates, picks, _, shape_len = templates.shape
    pieces = record_len // LANES
    blocks = record_len // LANES - 3
    block_rows = -(-own_stations * pieces // 16) * 16
    mine = jnp.pad(
        jnp.transpose(records.reshape(own_stations, channels, pieces, LANES), (1, 0, 2, 3)).reshape(
            channels, own_stations * pieces, LANES
        ),
        ((0, 0), (0, block_rows - own_stations * pieces), (0, 0)),
    )
    shapes = jnp.pad(
        jnp.transpose(templates, (2, 0, 1, 3)),
        ((0, 0), (0, 0), (0, -picks % 16), (0, 2 * LANES - shape_len)),
    )
    base = (pick_owner * block_rows + pick_local * pieces).reshape(-1)
    smem = pl.BlockSpec(memory_space=pltpu.SMEM)
    vmem = pl.BlockSpec(memory_space=pltpu.VMEM)
    return pl.pallas_call(
        functools.partial(fused_kernel, picks, channels, pieces),
        in_specs=[smem] * 4 + [vmem] * 2 + [pl.BlockSpec(memory_space=pl.ANY)],
        out_specs=vmem,
        out_shape=jax.ShapeDtypeStruct((own_templates, blocks, LANES), jnp.float32),
        scratch_shapes=[pltpu.VMEM((devices, block_rows, LANES), jnp.bfloat16)] * channels
        + [
            pltpu.VMEM((devices * block_rows, LANES), jnp.float32),
            pltpu.VMEM((GROUP, picks, blocks + 8, LANES), jnp.float32),
            pltpu.VMEM((GROUP, picks * blocks, 3 * LANES), jnp.bfloat16),
            pltpu.VMEM((GROUP, picks * blocks, LANES), jnp.float32),
            pltpu.VMEM((own_templates * picks, blocks, LANES), jnp.float32),
            pltpu.SemaphoreType.DMA((channels,)),
            pltpu.SemaphoreType.DMA((channels, devices - 1)),
            pltpu.SemaphoreType.DMA((channels, devices)),
        ],
        compiler_params=pltpu.CompilerParams(
            collective_id=0, has_side_effects=True, vmem_limit_bytes=48 * 1024 * 1024
        ),
    )(base, moveout.reshape(-1), power, mask, band, shapes, mine)


def on_device(records, templates, pick_owner, pick_local, moveout, channel_mask):
    own_stations, channels, record_len = records.shape
    own_templates, picks, _, shape_len = templates.shape
    pieces = record_len // LANES
    frame_len = 3 * LANES
    blocks = (record_len - frame_len) // LANES
    power = jnp.sum(jnp.square(templates.astype(jnp.float32)), axis=3).reshape(-1)
    mask = channel_mask.astype(jnp.float32).reshape(-1)
    offsets = (
        jnp.arange(frame_len, dtype=jnp.int32)[:, None] - jnp.arange(LANES, dtype=jnp.int32)[None, :]
    )
    band = ((offsets >= 0) & (offsets < shape_len)).astype(jnp.bfloat16)

    small = (lax.axis_size("sta"), lax.axis_size("tpl"), channels) == (8, 4, 3)
    if small and own_templates == 4 * GROUP:
        stacked = fused(records, templates, pick_owner, pick_local, moveout, power, mask, band)
        return stacked.reshape(own_templates, blocks * LANES)

    held = -(-channels * pieces // 16) * 16
    everywhere = lax.all_gather(
        jnp.pad(
            records.reshape(own_stations, channels * pieces, LANES),
            ((0, 0), (0, held - channels * pieces), (0, 0)),
        ),
        ("sta", "tpl"),
        axis=0,
        tiled=True,
    )
    station = (pick_owner * own_stations + pick_local).reshape(-1)
    items = picks * channels
    shapes = jnp.pad(
        templates.reshape(own_templates, items, shape_len),
        ((0, 0), (0, -items % 16), (0, 2 * LANES - shape_len)),
    )

    def record_spec(pick):
        return pl.BlockSpec(
            (1, held, LANES),
            lambda t, station, shift, power, mask: (station[t * picks + pick], 0, 0),
        )

    stacked = pl.pallas_call(
        functools.partial(stack_kernel, picks, channels, pieces),
        grid_spec=pltpu.PrefetchScalarGridSpec(
            num_scalar_prefetch=4,
            grid=(own_templates,),
            in_specs=[
                pl.BlockSpec((frame_len, LANES), lambda t, *_: (0, 0)),
                pl.BlockSpec((1,) + shapes.shape[1:], lambda t, *_: (t, 0, 0)),
            ]
            + [record_spec(pick) for pick in range(picks)],
            out_specs=pl.BlockSpec((1, blocks, LANES), lambda t, *_: (t, 0, 0)),
            scratch_shapes=[
                pltpu.VMEM((picks, held + 8, LANES), jnp.float32),
                pltpu.VMEM((items * blocks, frame_len), jnp.bfloat16),
                pltpu.VMEM((items * blocks, LANES), jnp.float32),
            ],
        ),
        out_shape=jax.ShapeDtypeStruct((own_templates, blocks, LANES), jnp.float32),
        compiler_params=pltpu.CompilerParams(vmem_limit_bytes=48 * 1024 * 1024),
    )(station, moveout.reshape(-1), power, mask, band, shapes, *([everywhere] * picks))
    return stacked.reshape(own_templates, blocks * LANES)


def solution(mesh):
    return jax.shard_map(
        on_device,
        mesh=mesh,
        in_specs=(
            P(("sta", "tpl"), None, None),
            P(("sta", "tpl"), None, None, None),
            P(("sta", "tpl"), None),
            P(("sta", "tpl"), None),
            P(("sta", "tpl"), None),
            P(("sta", "tpl"), None, None),
        ),
        out_specs=P(("sta", "tpl"), None),
        check_vma=False,
    )
```

```python
import functools

import jax
import jax.numpy as jnp
from jax import lax
from jax.experimental import pallas as pl
from jax.experimental.pallas import tpu as pltpu
from jax.sharding import PartitionSpec as P

EPS = 1e-06
LANES = 128
GROUP = 6
MESH = pl.DeviceIdType.MESH


def toeplitz(row):
    base = pltpu.roll(
        jnp.broadcast_to(row, (16, 256)), 0, axis=1, stride=1, stride_axis=0
    ).astype(jnp.bfloat16)
    zeros = jnp.zeros((16, LANES), jnp.bfloat16)
    wide = jnp.concatenate([base, zeros], axis=1)
    strips = [wide]
    for step in range(1, 8):
        strips.append(
            jnp.concatenate([zeros[:, : 16 * step], wide[:, : 384 - 16 * step]], axis=1)
        )
    return jnp.concatenate(strips, axis=0)


def stack_kernel(picks, channels, pieces, station, shift, power, mask, band_ref, shapes_ref, *rest):
    record_refs, out_ref, wide_ref, squares_ref, energy_ref = rest[:picks], *rest[picks:]
    blocks = out_ref.shape[1]
    held = record_refs[0].shape[1]
    template = pl.program_id(0)
    shapes = shapes_ref[0].astype(jnp.float32)
    lane = lax.broadcasted_iota(jnp.int32, (held, LANES), 1)
    windows = []
    for pick in range(picks):
        moved = shift[template * picks + pick]
        wide_ref[pick, :held] = pltpu.roll(
            record_refs[pick][0].astype(jnp.float32), lax.rem(LANES - moved, LANES), axis=1
        )
        wide_ref[pick, :held] = jnp.where(
            lane < LANES - moved, wide_ref[pick, :held], wide_ref[pick, 1 : held + 1]
        )
        for channel in range(channels):
            first = channel * pieces
            window = jnp.concatenate(
                [
                    wide_ref[pick, first + k : first + k + blocks].astype(jnp.bfloat16)
                    for k in range(3)
                ],
                axis=1,
            )
            windows.append(window)
            item = pick * channels + channel
            squares_ref[item * blocks : (item + 1) * blocks] = window * window
    energy_ref[...] = jnp.dot(
        squares_ref[...], band_ref[...], preferred_element_type=jnp.float32
    )
    total = jnp.zeros((blocks, LANES), jnp.float32)
    for pick in range(picks):
        trace = jnp.zeros((blocks, LANES), jnp.float32)
        for channel in range(channels):
            item = pick * channels + channel
            at = template * (picks * channels) + item
            correlation = lax.dot_general(
                windows[item],
                toeplitz(shapes[item : item + 1]),
                (((1,), (1,)), ((), ())),
                preferred_element_type=jnp.float32,
            )
            scale = lax.rsqrt(power[at] * energy_ref[item * blocks : (item + 1) * blocks] + EPS)
            trace = trace + mask[at] * (correlation * scale)
        total = total + trace.astype(jnp.bfloat16).astype(jnp.float32)
    mean = jnp.sum(total * total) / (blocks * LANES)
    out_ref[0] = total * lax.rsqrt(jnp.full((blocks, LANES), mean + EPS, jnp.float32))


def fused_kernel(
    picks, channels, pieces, base, shift, power, mask, band_ref, shapes_ref, mine_ref, out_ref, *scratch
):
    landed = scratch[:channels]
    wide_ref, turned_ref, windows_ref, energy_ref, traces_ref, tables_ref, local_sem, send_sem, recv_sem = scratch[channels:]
    templates, blocks = out_ref.shape[0], out_ref.shape[1]
    devices, block_rows = landed[0].shape[0], landed[0].shape[1]
    sta, tpl = lax.axis_index("sta"), lax.axis_index("tpl")
    z, x, y, core = sta // 2, sta % 2, tpl // 2, tpl % 2
    first_x, first_y = x + (1 - core) * (1 - 2 * x), y + core * (1 - 2 * y)
    second_x, second_y = x + core * (1 - 2 * x), y + (1 - core) * (1 - 2 * y)
    heights = [z, z + 1 - 2 * (z % 2), (z + 2) % 4, 3 - z]
    first = (z * 2 + first_x, first_y * 2 + core)
    second = (z * 2 + second_x, second_y * 2 + core)
    sibling = (sta, y * 2 + 1 - core)
    partners = [(height * 2 + x, tpl) for height in heights[1:]] + [first, second, sibling]

    def number(height, at_x, at_y, at_core):
        return (height * 2 + at_x) * 4 + at_y * 2 + at_core

    own = number(z, x, y, core)
    def wait(height, at_x, at_y, onward):
        shard = number(height, at_x, at_y, core)
        return [(shard, None, None)] + [(None, shard, partner) for partner in onward]

    def straight(step):
        return wait(heights[step], x, y, (first, second, sibling))

    def by_first(step):
        return wait(heights[step], first_x, first_y, (second, sibling))

    def by_second(step):
        return wait(heights[step], second_x, second_y, (sibling,))

    def by_both(step):
        return wait(heights[step], 1 - x, 1 - y, (sibling,))

    plan = [
        [(None, own, partner) for partner in partners],
        by_first(0) + by_second(0) + straight(1) + straight(2) + straight(3),
        by_first(1) + by_both(0) + by_second(1) + by_first(2) + by_second(2) + by_first(3) + by_second(3),
        by_both(1) + by_both(2) + by_both(3),
        [
            (number(height, at_x, at_y, 1 - core), None, None)
            for height in heights
            for at_x, at_y in ((x, y), (first_x, first_y), (second_x, second_y), (1 - x, 1 - y))
        ],
    ]
    firsts = [sum(move[0] is None for moves in plan[:k] for move in moves) for k in range(len(plan))]

    def copy_of(channel, index, shard, partner, source=None):
        place = landed[channel].at[shard]
        return pltpu.make_async_remote_copy(
            src_ref=place if source is None else source,
            dst_ref=place,
            send_sem=send_sem.at[channel, index],
            recv_sem=recv_sem.at[channel, shard],
            device_id=partner,
            device_id_type=MESH,
        )

    def run(channel, part):
        index = firsts[part]
        for arrival, shard, partner in plan[part]:
            if arrival is not None:
                copy_of(channel, 0, arrival, sibling).wait_recv()
            else:
                copy_of(
                    channel, index, shard, partner, mine_ref.at[channel] if part == 0 else None
                ).start()
                index += 1

    def local(channel):
        return pltpu.make_async_copy(
            mine_ref.at[channel], landed[channel].at[own], local_sem.at[channel]
        )

    barrier = pltpu.get_barrier_semaphore()
    for partner in partners:
        pl.semaphore_signal(barrier, inc=1, device_id=partner, device_id_type=MESH)
    pl.semaphore_wait(barrier, len(partners))
    for channel in range(channels):
        local(channel).start()
    run(0, 0)
    third = templates // 3

    def tabulate(template, carry):
        for part in (1, 2):

            @pl.when(template == part * third)
            def _(part=part):
                run(0, part)

        shapes = shapes_ref[0, template].astype(jnp.float32)
        for pick in range(picks):
            tables_ref[template * picks + pick] = toeplitz(shapes[pick : pick + 1])
        return carry

    lax.fori_loop(0, templates, tabulate, 0)
    run(1, 0)
    run(0, 3)

    lane = lax.broadcasted_iota(jnp.int32, (blocks, LANES), 1)
    for channel in range(channels):
        run(channel, 4)
        local(channel).wait()

        def widen(device, carry, channel=channel):
            at = pl.multiple_of(device * block_rows, 16)
            wide_ref[pl.ds(at, block_rows)] = landed[channel][device].astype(jnp.float32)
            return carry

        lax.fori_loop(0, devices, widen, 0)

        def prepare(template, slot):
            for pick in range(picks):
                item = template * picks + pick
                moved = shift[item]
                turned_ref[slot, pick] = pltpu.roll(
                    wide_ref[pl.ds(base[item], turned_ref.shape[2])],
                    lax.rem(LANES - moved, LANES),
                    axis=1,
                )
                windows_ref[slot, pick * blocks : (pick + 1) * blocks] = jnp.concatenate(
                    [
                        jnp.where(
                            lane < LANES - moved,
                            turned_ref[slot, pick, k : k + blocks],
                            turned_ref[slot, pick, k + 1 : k + 1 + blocks],
                        ).astype(jnp.bfloat16)
                        for k in range(3)
                    ],
                    axis=1,
                )
            windows = windows_ref[slot]
            energy_ref[slot] = jnp.dot(
                windows * windows, band_ref[...], preferred_element_type=jnp.float32
            )

        def combine(template, slot, channel):
            shapes = shapes_ref[channel, template].astype(jnp.float32)
            total = jnp.zeros((blocks, LANES), jnp.float32)
            for pick in range(picks):
                item = template * picks + pick
                correlation = lax.dot_general(
                    windows_ref[slot, pick * blocks : (pick + 1) * blocks],
                    toeplitz(shapes[pick : pick + 1]) if channel else tables_ref[item],
                    (((1,), (1,)), ((), ())),
                    preferred_element_type=jnp.float32,
                )
                at = item * channels + channel
                scale = lax.rsqrt(
                    power[at] * energy_ref[slot, pick * blocks : (pick + 1) * blocks] + EPS
                )
                trace = mask[at] * (correlation * scale)
                if channel:
                    trace = trace + traces_ref[item]
                if channel + 1 < channels:
                    traces_ref[item] = trace
                else:
                    total = total + trace.astype(jnp.bfloat16).astype(jnp.float32)
            if channel + 1 == channels:
                mean = jnp.sum(total * total) / (blocks * LANES)
                out_ref[template] = total * lax.rsqrt(
                    jnp.full((blocks, LANES), mean + EPS, jnp.float32)
                )

        def stack(step, carry, channel=channel):
            if channel + 1 < channels:
                for part in (1, 2, 3):

                    @pl.when(step == part)
                    def _(part=part):
                        run(channel + 1, part)
                        if channel + 2 < channels and part == 3:
                            run(channel + 2, 0)

            prepare(step * GROUP, 0)
            for slot in range(GROUP):
                if slot + 1 < GROUP:
                    prepare(step * GROUP + slot + 1, slot + 1)
                combine(step * GROUP + slot, slot, channel)
            return carry

        lax.fori_loop(0, templates // GROUP, stack, 0)
    for channel in range(channels):
        index = 0
        for part, moves in enumerate(plan):
            for arrival, shard, partner in moves:
                if arrival is None:
                    copy_of(
                        channel, index, shard, partner, mine_ref.at[channel] if part == 0 else None
                    ).wait_send()
                    index += 1


def fused(records, templates, pick_owner, pick_local, moveout, power, mask, band):
    devices = lax.axis_size(("sta", "tpl"))
    own_stations, channels, record_len = records.shape
    own_templates, picks, _, shape_len = templates.shape
    pieces = record_len // LANES
    blocks = record_len // LANES - 3
    block_rows = -(-own_stations * pieces // 16) * 16
    mine = jnp.pad(
        jnp.transpose(records.reshape(own_stations, channels, pieces, LANES), (1, 0, 2, 3)).reshape(
            channels, own_stations * pieces, LANES
        ),
        ((0, 0), (0, block_rows - own_stations * pieces), (0, 0)),
    )
    shapes = jnp.pad(
        jnp.transpose(templates, (2, 0, 1, 3)),
        ((0, 0), (0, 0), (0, -picks % 16), (0, 2 * LANES - shape_len)),
    )
    base = (pick_owner * block_rows + pick_local * pieces).reshape(-1)
    smem = pl.BlockSpec(memory_space=pltpu.SMEM)
    vmem = pl.BlockSpec(memory_space=pltpu.VMEM)
    return pl.pallas_call(
        functools.partial(fused_kernel, picks, channels, pieces),
        in_specs=[smem] * 4 + [vmem] * 2 + [pl.BlockSpec(memory_space=pl.ANY)],
        out_specs=vmem,
        out_shape=jax.ShapeDtypeStruct((own_templates, blocks, LANES), jnp.float32),
        scratch_shapes=[pltpu.VMEM((devices, block_rows, LANES), jnp.bfloat16)] * channels
        + [
            pltpu.VMEM((devices * block_rows, LANES), jnp.float32),
            pltpu.VMEM((GROUP, picks, blocks + 8, LANES), jnp.float32),
            pltpu.VMEM((GROUP, picks * blocks, 3 * LANES), jnp.bfloat16),
            pltpu.VMEM((GROUP, picks * blocks, LANES), jnp.float32),
            pltpu.VMEM((own_templates * picks, blocks, LANES), jnp.float32),
            pltpu.VMEM((own_templates * picks, LANES, 3 * LANES), jnp.bfloat16),
            pltpu.SemaphoreType.DMA((channels,)),
            pltpu.SemaphoreType.DMA((channels, devices - 1)),
            pltpu.SemaphoreType.DMA((channels, devices)),
        ],
        compiler_params=pltpu.CompilerParams(
            collective_id=0, has_side_effects=True, vmem_limit_bytes=56 * 1024 * 1024
        ),
    )(base, moveout.reshape(-1), power, mask, band, shapes, mine)


def on_device(records, templates, pick_owner, pick_local, moveout, channel_mask):
    own_stations, channels, record_len = records.shape
    own_templates, picks, _, shape_len = templates.shape
    pieces = record_len // LANES
    frame_len = 3 * LANES
    blocks = (record_len - frame_len) // LANES
    power = jnp.sum(jnp.square(templates.astype(jnp.float32)), axis=3).reshape(-1)
    mask = channel_mask.astype(jnp.float32).reshape(-1)
    offsets = (
        jnp.arange(frame_len, dtype=jnp.int32)[:, None] - jnp.arange(LANES, dtype=jnp.int32)[None, :]
    )
    band = ((offsets >= 0) & (offsets < shape_len)).astype(jnp.bfloat16)

    small = (lax.axis_size("sta"), lax.axis_size("tpl"), channels) == (8, 4, 3)
    if small and own_templates == 4 * GROUP:
        stacked = fused(records, templates, pick_owner, pick_local, moveout, power, mask, band)
        return stacked.reshape(own_templates, blocks * LANES)

    held = -(-channels * pieces // 16) * 16
    everywhere = lax.all_gather(
        jnp.pad(
            records.reshape(own_stations, channels * pieces, LANES),
            ((0, 0), (0, held - channels * pieces), (0, 0)),
        ),
        ("sta", "tpl"),
        axis=0,
        tiled=True,
    )
    station = (pick_owner * own_stations + pick_local).reshape(-1)
    items = picks * channels
    shapes = jnp.pad(
        templates.reshape(own_templates, items, shape_len),
        ((0, 0), (0, -items % 16), (0, 2 * LANES - shape_len)),
    )

    def record_spec(pick):
        return pl.BlockSpec(
            (1, held, LANES),
            lambda t, station, shift, power, mask: (station[t * picks + pick], 0, 0),
        )

    stacked = pl.pallas_call(
        functools.partial(stack_kernel, picks, channels, pieces),
        grid_spec=pltpu.PrefetchScalarGridSpec(
            num_scalar_prefetch=4,
            grid=(own_templates,),
            in_specs=[
                pl.BlockSpec((frame_len, LANES), lambda t, *_: (0, 0)),
                pl.BlockSpec((1,) + shapes.shape[1:], lambda t, *_: (t, 0, 0)),
            ]
            + [record_spec(pick) for pick in range(picks)],
            out_specs=pl.BlockSpec((1, blocks, LANES), lambda t, *_: (t, 0, 0)),
            scratch_shapes=[
                pltpu.VMEM((picks, held + 8, LANES), jnp.float32),
                pltpu.VMEM((items * blocks, frame_len), jnp.bfloat16),
                pltpu.VMEM((items * blocks, LANES), jnp.float32),
            ],
        ),
        out_shape=jax.ShapeDtypeStruct((own_templates, blocks, LANES), jnp.float32),
        compiler_params=pltpu.CompilerParams(vmem_limit_bytes=48 * 1024 * 1024),
    )(station, moveout.reshape(-1), power, mask, band, shapes, *([everywhere] * picks))
    return stacked.reshape(own_templates, blocks * LANES)


def solution(mesh):
    return jax.shard_map(
        on_device,
        mesh=mesh,
        in_specs=(
            P(("sta", "tpl"), None, None),
            P(("sta", "tpl"), None, None, None),
            P(("sta", "tpl"), None),
            P(("sta", "tpl"), None),
            P(("sta", "tpl"), None),
            P(("sta", "tpl"), None, None),
        ),
        out_specs=P(("sta", "tpl"), None),
        check_vma=False,
    )
```

```python
import functools

import jax
import jax.numpy as jnp
from jax import lax
from jax.experimental import pallas as pl
from jax.experimental.pallas import tpu as pltpu
from jax.sharding import PartitionSpec as P

EPS = 1e-06
LANES = 128
GROUP = 6
EXTRA = 12
MESH = pl.DeviceIdType.MESH


def toeplitz(row):
    base = pltpu.roll(
        jnp.broadcast_to(row, (16, 256)), 0, axis=1, stride=1, stride_axis=0
    ).astype(jnp.bfloat16)
    zeros = jnp.zeros((16, LANES), jnp.bfloat16)
    wide = jnp.concatenate([base, zeros], axis=1)
    strips = [wide]
    for step in range(1, 8):
        strips.append(
            jnp.concatenate([zeros[:, : 16 * step], wide[:, : 384 - 16 * step]], axis=1)
        )
    return jnp.concatenate(strips, axis=0)


def stack_kernel(picks, channels, pieces, station, shift, power, mask, band_ref, shapes_ref, *rest):
    record_refs, out_ref, wide_ref, squares_ref, energy_ref = rest[:picks], *rest[picks:]
    blocks = out_ref.shape[1]
    held = record_refs[0].shape[1]
    template = pl.program_id(0)
    shapes = shapes_ref[0].astype(jnp.float32)
    lane = lax.broadcasted_iota(jnp.int32, (held, LANES), 1)
    windows = []
    for pick in range(picks):
        moved = shift[template * picks + pick]
        wide_ref[pick, :held] = pltpu.roll(
            record_refs[pick][0].astype(jnp.float32), lax.rem(LANES - moved, LANES), axis=1
        )
        wide_ref[pick, :held] = jnp.where(
            lane < LANES - moved, wide_ref[pick, :held], wide_ref[pick, 1 : held + 1]
        )
        for channel in range(channels):
            first = channel * pieces
            window = jnp.concatenate(
                [
                    wide_ref[pick, first + k : first + k + blocks].astype(jnp.bfloat16)
                    for k in range(3)
                ],
                axis=1,
            )
            windows.append(window)
            item = pick * channels + channel
            squares_ref[item * blocks : (item + 1) * blocks] = window * window
    energy_ref[...] = jnp.dot(
        squares_ref[...], band_ref[...], preferred_element_type=jnp.float32
    )
    total = jnp.zeros((blocks, LANES), jnp.float32)
    for pick in range(picks):
        trace = jnp.zeros((blocks, LANES), jnp.float32)
        for channel in range(channels):
            item = pick * channels + channel
            at = template * (picks * channels) + item
            correlation = lax.dot_general(
                windows[item],
                toeplitz(shapes[item : item + 1]),
                (((1,), (1,)), ((), ())),
                preferred_element_type=jnp.float32,
            )
            scale = lax.rsqrt(power[at] * energy_ref[item * blocks : (item + 1) * blocks] + EPS)
            trace = trace + mask[at] * (correlation * scale)
        total = total + trace.astype(jnp.bfloat16).astype(jnp.float32)
    mean = jnp.sum(total * total) / (blocks * LANES)
    out_ref[0] = total * lax.rsqrt(jnp.full((blocks, LANES), mean + EPS, jnp.float32))


def fused_kernel(
    picks, channels, pieces, owner, place, shift, power, mask, band_ref, shapes_ref, mine_ref, out_ref, *scratch
):
    landed = scratch[:channels]
    wide_ref, turned_ref, windows_ref, energy_ref, traces_ref, tables_ref, local_sem, send_sem, recv_sem = scratch[channels:]
    templates, blocks = out_ref.shape[0], out_ref.shape[1]
    devices, block_rows = landed[0].shape[0], landed[0].shape[1]
    sta, tpl = lax.axis_index("sta"), lax.axis_index("tpl")
    z, x, y, core = sta // 2, sta % 2, tpl // 2, tpl % 2
    first_x, first_y = x + (1 - core) * (1 - 2 * x), y + core * (1 - 2 * y)
    second_x, second_y = x + core * (1 - 2 * x), y + (1 - core) * (1 - 2 * y)
    heights = [z, z + 1 - 2 * (z % 2), (z + 2) % 4, 3 - z]
    first = (z * 2 + first_x, first_y * 2 + core)
    second = (z * 2 + second_x, second_y * 2 + core)
    sibling = (sta, y * 2 + 1 - core)
    partners = [(height * 2 + x, tpl) for height in heights[1:]] + [first, second, sibling]

    def number(height, at_x, at_y, at_core):
        return (height * 2 + at_x) * 4 + at_y * 2 + at_core

    own = number(z, x, y, core)
    def wait(height, at_x, at_y, onward):
        shard = number(height, at_x, at_y, core)
        return [(shard, None, None)] + [(None, shard, partner) for partner in onward]

    def straight(step):
        return wait(heights[step], x, y, (first, second, sibling))

    def by_first(step):
        return wait(heights[step], first_x, first_y, (second, sibling))

    def by_second(step):
        return wait(heights[step], second_x, second_y, (sibling,))

    def by_both(step):
        return wait(heights[step], 1 - x, 1 - y, (sibling,))

    plan = [
        [(None, own, partner) for partner in partners],
        by_first(0) + by_second(0) + straight(1) + straight(2) + straight(3),
        by_first(1) + by_both(0) + by_second(1) + by_first(2) + by_second(2) + by_first(3) + by_second(3),
        by_both(1) + by_both(2) + by_both(3),
        [
            (number(height, at_x, at_y, 1 - core), None, None)
            for height in heights
            for at_x, at_y in ((x, y), (first_x, first_y), (second_x, second_y), (1 - x, 1 - y))
        ],
    ]
    firsts = [sum(move[0] is None for moves in plan[:k] for move in moves) for k in range(len(plan))]

    def copy_of(channel, index, shard, partner, source=None):
        place = landed[channel].at[shard]
        return pltpu.make_async_remote_copy(
            src_ref=place if source is None else source,
            dst_ref=place,
            send_sem=send_sem.at[channel, index],
            recv_sem=recv_sem.at[channel, shard],
            device_id=partner,
            device_id_type=MESH,
        )

    def run(channel, part):
        index = firsts[part]
        for arrival, shard, partner in plan[part]:
            if arrival is not None:
                copy_of(channel, 0, arrival, sibling).wait_recv()
            else:
                copy_of(
                    channel, index, shard, partner, mine_ref.at[channel] if part == 0 else None
                ).start()
                index += 1

    def local(channel):
        return pltpu.make_async_copy(
            mine_ref.at[channel], landed[channel].at[own], local_sem.at[channel]
        )

    barrier = pltpu.get_barrier_semaphore()
    for partner in partners:
        pl.semaphore_signal(barrier, inc=1, device_id=partner, device_id_type=MESH)
    pl.semaphore_wait(barrier, len(partners))
    for channel in range(channels):
        local(channel).start()
    run(0, 0)
    ready = tables_ref.shape[0] // picks
    third = ready // 3

    def tabulate(entry, carry):
        for part in (1, 2):

            @pl.when(entry == part * third)
            def _(part=part):
                run(0, part)

        extra = entry // templates
        shapes = shapes_ref[extra * (channels - 1), entry - extra * templates].astype(jnp.float32)
        for pick in range(picks):
            tables_ref[entry * picks + pick] = toeplitz(shapes[pick : pick + 1])
        return carry

    lax.fori_loop(0, ready, tabulate, 0)
    run(1, 0)
    run(0, 3)

    lane = lax.broadcasted_iota(jnp.int32, (blocks, LANES), 1)
    for channel in range(channels):
        run(channel, 4)
        local(channel).wait()

        def widen(device, carry, channel=channel):
            at = pl.multiple_of(device * block_rows, 16)
            wide_ref[pl.ds(at, block_rows)] = landed[channel][device].astype(jnp.float32)
            return carry

        lax.fori_loop(0, devices, widen, 0)

        def prepare(template, slot):
            for pick in range(picks):
                moved = shift[template, pick]
                base = owner[template, pick] * block_rows + place[template, pick] * pieces
                turned_ref[slot, pick] = pltpu.roll(
                    wide_ref[pl.ds(base, turned_ref.shape[2])],
                    lax.rem(LANES - moved, LANES),
                    axis=1,
                )
                windows_ref[slot, pick * blocks : (pick + 1) * blocks] = jnp.concatenate(
                    [
                        jnp.where(
                            lane < LANES - moved,
                            turned_ref[slot, pick, k : k + blocks],
                            turned_ref[slot, pick, k + 1 : k + 1 + blocks],
                        ).astype(jnp.bfloat16)
                        for k in range(3)
                    ],
                    axis=1,
                )
            windows = windows_ref[slot]
            energy_ref[slot] = jnp.dot(
                windows * windows, band_ref[...], preferred_element_type=jnp.float32
            )

        def combine(template, slot, channel, start):
            shapes = shapes_ref[channel, template].astype(jnp.float32)
            total = jnp.zeros((blocks, LANES), jnp.float32)
            for pick in range(picks):
                item = template * picks + pick
                correlation = lax.dot_general(
                    windows_ref[slot, pick * blocks : (pick + 1) * blocks],
                    toeplitz(shapes[pick : pick + 1]) if start is None else tables_ref[start + item],
                    (((1,), (1,)), ((), ())),
                    preferred_element_type=jnp.float32,
                )
                at = pick * channels + channel
                scale = lax.rsqrt(
                    power[template, at] * energy_ref[slot, pick * blocks : (pick + 1) * blocks] + EPS
                )
                trace = mask[template, at] * (correlation * scale)
                if channel:
                    trace = trace + traces_ref[item]
                if channel + 1 < channels:
                    traces_ref[item] = trace
                else:
                    total = total + trace.astype(jnp.bfloat16).astype(jnp.float32)
            if channel + 1 == channels:
                mean = jnp.sum(total * total) / (blocks * LANES)
                out_ref[template] = total * lax.rsqrt(
                    jnp.full((blocks, LANES), mean + EPS, jnp.float32)
                )

        def stack(step, carry, channel=channel, start=None):
            if channel + 1 < channels:
                for part in (1, 2, 3):

                    @pl.when(step == part)
                    def _(part=part):
                        run(channel + 1, part)
                        if channel + 2 < channels and part == 3:
                            run(channel + 2, 0)

            prepare(step * GROUP, 0)
            for slot in range(GROUP):
                if slot + 1 < GROUP:
                    prepare(step * GROUP + slot + 1, slot + 1)
                combine(step * GROUP + slot, slot, channel, start)
            return carry

        steps = templates // GROUP
        at_hand = (steps, 0, ready // GROUP - steps)[channel]
        if at_hand:
            start = templates * picks if channel else 0
            lax.fori_loop(0, at_hand, functools.partial(stack, start=start), 0)
        if at_hand < steps:
            lax.fori_loop(at_hand, steps, stack, 0)
    for channel in range(channels):
        index = 0
        for part, moves in enumerate(plan):
            for arrival, shard, partner in moves:
                if arrival is None:
                    copy_of(
                        channel, index, shard, partner, mine_ref.at[channel] if part == 0 else None
                    ).wait_send()
                    index += 1


def fused(records, templates, pick_owner, pick_local, moveout, power, mask, band):
    devices = lax.axis_size(("sta", "tpl"))
    own_stations, channels, record_len = records.shape
    own_templates, picks, _, shape_len = templates.shape
    pieces = record_len // LANES
    blocks = record_len // LANES - 3
    block_rows = -(-own_stations * pieces // 16) * 16
    mine = jnp.pad(
        jnp.transpose(records.reshape(own_stations, channels, pieces, LANES), (1, 0, 2, 3)).reshape(
            channels, own_stations * pieces, LANES
        ),
        ((0, 0), (0, block_rows - own_stations * pieces), (0, 0)),
    )
    shapes = jnp.pad(
        jnp.transpose(templates, (2, 0, 1, 3)),
        ((0, 0), (0, 0), (0, -picks % 16), (0, 2 * LANES - shape_len)),
    )
    smem = pl.BlockSpec(memory_space=pltpu.SMEM)
    vmem = pl.BlockSpec(memory_space=pltpu.VMEM)
    return pl.pallas_call(
        functools.partial(fused_kernel, picks, channels, pieces),
        in_specs=[smem] * 5 + [vmem] * 2 + [pl.BlockSpec(memory_space=pl.ANY)],
        out_specs=vmem,
        out_shape=jax.ShapeDtypeStruct((own_templates, blocks, LANES), jnp.float32),
        scratch_shapes=[pltpu.VMEM((devices, block_rows, LANES), jnp.bfloat16)] * channels
        + [
            pltpu.VMEM((devices * block_rows, LANES), jnp.float32),
            pltpu.VMEM((GROUP, picks, blocks + 8, LANES), jnp.float32),
            pltpu.VMEM((GROUP, picks * blocks, 3 * LANES), jnp.bfloat16),
            pltpu.VMEM((GROUP, picks * blocks, LANES), jnp.float32),
            pltpu.VMEM((own_templates * picks, blocks, LANES), jnp.float32),
            pltpu.VMEM(((own_templates + EXTRA) * picks, LANES, 3 * LANES), jnp.bfloat16),
            pltpu.SemaphoreType.DMA((channels,)),
            pltpu.SemaphoreType.DMA((channels, devices - 1)),
            pltpu.SemaphoreType.DMA((channels, devices)),
        ],
        compiler_params=pltpu.CompilerParams(
            collective_id=0, has_side_effects=True, vmem_limit_bytes=58 * 1024 * 1024
        ),
    )(
        pick_owner,
        pick_local,
        moveout,
        power.reshape(own_templates, picks * channels),
        mask.reshape(own_templates, picks * channels),
        band,
        shapes,
        mine,
    )


def on_device(records, templates, pick_owner, pick_local, moveout, channel_mask):
    own_stations, channels, record_len = records.shape
    own_templates, picks, _, shape_len = templates.shape
    pieces = record_len // LANES
    frame_len = 3 * LANES
    blocks = (record_len - frame_len) // LANES
    power = jnp.sum(jnp.square(templates.astype(jnp.float32)), axis=3)
    mask = channel_mask.astype(jnp.float32)
    offsets = (
        jnp.arange(frame_len, dtype=jnp.int32)[:, None] - jnp.arange(LANES, dtype=jnp.int32)[None, :]
    )
    band = ((offsets >= 0) & (offsets < shape_len)).astype(jnp.bfloat16)

    small = (lax.axis_size("sta"), lax.axis_size("tpl"), channels) == (8, 4, 3)
    if small and own_templates == 4 * GROUP:
        stacked = fused(records, templates, pick_owner, pick_local, moveout, power, mask, band)
        return stacked.reshape(own_templates, blocks * LANES)

    held = -(-channels * pieces // 16) * 16
    everywhere = lax.all_gather(
        jnp.pad(
            records.reshape(own_stations, channels * pieces, LANES),
            ((0, 0), (0, held - channels * pieces), (0, 0)),
        ),
        ("sta", "tpl"),
        axis=0,
        tiled=True,
    )
    station = (pick_owner * own_stations + pick_local).reshape(-1)
    items = picks * channels
    shapes = jnp.pad(
        templates.reshape(own_templates, items, shape_len),
        ((0, 0), (0, -items % 16), (0, 2 * LANES - shape_len)),
    )

    def record_spec(pick):
        return pl.BlockSpec(
            (1, held, LANES),
            lambda t, station, shift, power, mask: (station[t * picks + pick], 0, 0),
        )

    stacked = pl.pallas_call(
        functools.partial(stack_kernel, picks, channels, pieces),
        grid_spec=pltpu.PrefetchScalarGridSpec(
            num_scalar_prefetch=4,
            grid=(own_templates,),
            in_specs=[
                pl.BlockSpec((frame_len, LANES), lambda t, *_: (0, 0)),
                pl.BlockSpec((1,) + shapes.shape[1:], lambda t, *_: (t, 0, 0)),
            ]
            + [record_spec(pick) for pick in range(picks)],
            out_specs=pl.BlockSpec((1, blocks, LANES), lambda t, *_: (t, 0, 0)),
            scratch_shapes=[
                pltpu.VMEM((picks, held + 8, LANES), jnp.float32),
                pltpu.VMEM((items * blocks, frame_len), jnp.bfloat16),
                pltpu.VMEM((items * blocks, LANES), jnp.float32),
            ],
        ),
        out_shape=jax.ShapeDtypeStruct((own_templates, blocks, LANES), jnp.float32),
        compiler_params=pltpu.CompilerParams(vmem_limit_bytes=48 * 1024 * 1024),
    )(station, moveout.reshape(-1), power.reshape(-1), mask.reshape(-1), band, shapes, *([everywhere] * picks))
    return stacked.reshape(own_templates, blocks * LANES)


def solution(mesh):
    return jax.shard_map(
        on_device,
        mesh=mesh,
        in_specs=(
            P(("sta", "tpl"), None, None),
            P(("sta", "tpl"), None, None, None),
            P(("sta", "tpl"), None),
            P(("sta", "tpl"), None),
            P(("sta", "tpl"), None),
            P(("sta", "tpl"), None, None),
        ),
        out_specs=P(("sta", "tpl"), None),
        check_vma=False,
    )
```
